32 devices in a mesh: frag: 2 (over y), bas: 4 (over z), aux: 2 (over x), orb: 2 (over core).
Axes of the slice: x: 2, y: 2, z: 4, core: 2. Of those that a mesh axis runs over, the one named last changes fastest.
Arguments:
- tiles: bfloat16 [128, 1024, 128], P(('frag', 'bas', 'aux')), parts along dimension 0, may hold values from -0.125 to 0.125
- screen: int32 [128, 3], P(('frag', 'bas', 'aux')), parts along dimension 0, may hold values from 0 to 95, as said below
- counts: int32 [16, 1], P(('frag', 'bas', 'aux')), parts along dimension 0, may hold values from 1 to 8, as said below
- orbitals: bfloat16 [24576, 128], P(('frag', 'bas'), 'orb'), parts along dimension 0, may hold values from -0.5 to 0.5
Outputs:
- exchange_block: float32 [512, 256], P(('frag', 'bas'), ('aux', 'orb')), parts along dimension 0
The draws below stay inside these ranges and needn't reach their ends.
There are 2 independent parts, one for each index of `frag`. The reference program is written for one: setup_inputs(seed, part) draws one part's arguments, and reference() takes and returns one part's arrays. A program takes and returns all parts, laid end to end along the dimension named above; each array names one. Nothing has to cross between parts.
Inputs may be any that keep to these rules, and one draw needn't show every extreme that they name: `screen`: each device's list names 8 different (block, row group, auxiliary block) triples; column 0 lies in 0 to 95, column 1 in 0 to 7, column 2 in 0 to 1. `counts`: slots at or beyond their device's count are not significant and are ignored, tiles and list entries alike; some device holds exactly 8 significant slots.
All inputs are finite; a program needn't handle non-finite values.
Results may differ from the reference program's by a relative error of at most 0.0003.
Values may be sent and summed in bfloat16 or wider, within the bound.
No kernel may reach another device: no remote copies, remote signals or barrier semaphores. Data moves between devices by JAX's collectives and lax.ppermute only.
A program may use at most 64 MiB of HBM per device.

```python
import jax
import jax.numpy as jnp
from jax import lax

NB = 12288
LB = 128
PB = 128
PBLK = 2
TM = 8
MSUB = 8
CAP = 8
ORBS = 128
N_BAS = 4
N_AUX = 2


def draw_screen(key, part):
    key = jax.random.fold_in(key, 11)
    combos = NB // LB * MSUB * PBLK
    subkeys = jax.random.split(key, N_BAS * N_AUX)
    picked = jax.vmap(lambda one_key: jax.random.permutation(one_key, combos)[:CAP])(subkeys)
    picked = picked.reshape(-1).astype(jnp.int32)
    lblock = picked // (MSUB * PBLK)
    remain = picked % (MSUB * PBLK)
    return jnp.stack([lblock, remain // PBLK, remain % PBLK], axis=1).astype(jnp.int32)


def draw_counts(key, part):
    key = jax.random.fold_in(key, 23)
    key_one, key_two, key_three = jax.random.split(key, 3)
    device_count = N_BAS * N_AUX
    chosen = jax.random.randint(key_one, (device_count,), 1, CAP + 1)
    others = jax.random.randint(key_two, (device_count,), 1, CAP + 1)
    busiest = jax.random.randint(key_three, (), 0, device_count)
    number = jnp.minimum(chosen, others)
    number = jnp.where(jnp.arange(device_count) == busiest, CAP, number)
    return number.reshape(device_count, 1).astype(jnp.int32)


def steps_of(key, dims, cuts, least, high):
    def one(dim, parts):
        heights = jax.random.uniform(jax.random.fold_in(jax.random.fold_in(key, 6), dim), (parts,), jnp.float32, least / len(cuts), high / len(cuts))
        return jnp.repeat(jnp.exp(heights), dims[dim] // parts).reshape((-1,) + (1,) * (len(dims) - dim - 1))

    factor_of = one(*cuts[0])
    for cut in cuts[1:]:
        factor_of = factor_of * one(*cut)
    return factor_of


def centred(key, dims, scale, bound, cuts=(), dtype=jnp.bfloat16):
    factor_of = steps_of(key, dims, cuts, -0.22, 0.18) if cuts else 1.0
    values = jax.random.normal(key, dims, jnp.float32) * scale * factor_of
    return jnp.minimum(jnp.maximum(values, -bound), bound).astype(dtype)


def setup_inputs(seed: int = 0, part: int = 0) -> dict:
    streams_of = jax.random.split(jax.random.key(seed), 5)
    own_keys = jax.random.split(jax.random.fold_in(streams_of[4], part), 5)
    return {
        "tiles": centred(own_keys[0], (N_BAS * N_AUX * CAP, PB * TM, LB), ((N_AUX * PB * ORBS * CAP / (3.0 * MSUB)) ** -0.5), 0.125, ((0, 8),)),
        "screen": draw_screen(jax.random.fold_in(jax.random.fold_in(streams_of[4], part), 71), part),
        "counts": draw_counts(jax.random.fold_in(jax.random.fold_in(streams_of[4], part), 71), part),
        "orbitals": centred(own_keys[3], (NB, ORBS), LB ** -0.5, 0.5, ((0, 4), (1, 2))),
    }


def reference(tiles, screen, counts, orbitals):
    device_count = N_BAS * N_AUX
    tile_sets = tiles.reshape(device_count, CAP, PB * TM, LB)
    lists = screen.reshape(device_count, CAP, 3)
    orbital_blocks = orbitals.reshape(NB // LB, LB, ORBS)

    def one_device(carry, item):
        tile_set, entries, number = item
        chosen = orbital_blocks[entries[:, 0]]
        products = jnp.einsum("srl,sli->sri", tile_set.astype(jnp.float32), chosen.astype(jnp.float32), precision=lax.Precision.HIGHEST)
        active = (jnp.arange(CAP) < number[0]).astype(jnp.float32)
        row_select = (entries[:, 1:2] == jnp.arange(MSUB)[None, :]).astype(jnp.float32) * active[:, None]
        aux_select = (entries[:, 2:3] == jnp.arange(PBLK)[None, :]).astype(jnp.float32)
        products = products.reshape(CAP, PB, TM, ORBS)
        placed = jnp.einsum("sptj,sa,sb->apbtj", products, aux_select, row_select, precision=lax.Precision.HIGHEST)
        return carry, placed.reshape(PBLK * PB, MSUB * TM, ORBS).astype(jnp.bfloat16)

    _, halves = lax.scan(one_device, jnp.float32(0.0), (tile_sets, lists, counts))
    halves = halves.reshape(N_BAS, N_AUX, PBLK * PB, MSUB * TM, ORBS)
    per_slab = jnp.transpose(halves, (1, 0, 3, 2, 4)).reshape(N_AUX, N_BAS * MSUB * TM, PBLK * PB * ORBS)

    def add_slab(total, rows):
        wide = rows.astype(jnp.float32)
        return total + jnp.dot(wide, wide.T, precision=lax.Precision.HIGHEST), None

    window = N_BAS * MSUB * TM
    result, _ = lax.scan(add_slab, jnp.zeros((window, window), jnp.float32), per_slab)
    return result
```

```python
import functools

import jax
import jax.numpy as jnp
from jax import lax
from jax.experimental import pallas as pl
from jax.experimental.pallas import tpu as pltpu
from jax.sharding import PartitionSpec as P

PBLK = 2
TM = 8
MSUB = 8
ROWS = MSUB * TM
VMEM_LIMIT = 40 * 1024 * 1024


def shift(x, axis, step, size):
    return lax.ppermute(x, axis, [(i, (i + step) % size) for i in range(size)])


def swap(x, axis, size):
    return lax.ppermute(x, axis, [(i, i ^ 1) for i in range(size)])


def vmem():
    return pl.BlockSpec(memory_space=pltpu.VMEM)


def smem():
    return pl.BlockSpec(memory_space=pltpu.SMEM)


def select_kernel(n_bas, blocks, where_ref, meta_ref, *refs):
    own, pieces, out_ref = refs[0], refs[1:-1], refs[-1]
    depth = own.shape[0] // 2
    slots = meta_ref.shape[1]
    me = where_ref[0]

    def one(index, carry):
        block = meta_ref[index // slots, index % slots, 0]
        owner = block // blocks
        back = lax.rem(me - owner + n_bas, n_bas)
        lanes = pl.ds(pl.multiple_of((block - owner * blocks) * 128, 128), 128)

        @pl.when(back == 0)
        def _():
            out_ref[index] = own[:, lanes]

        for step in range(1, n_bas):

            @pl.when(back == step)
            def _(step=step):
                out_ref[index, :depth, :] = pieces[2 * step - 2][:, lanes]
                out_ref[index, depth:, :] = pieces[2 * step - 1][:, lanes]

        return carry

    lax.fori_loop(0, n_bas * slots, one, 0)


def product_kernel(step, meta_ref, tile_ref, mine_ref, other_ref, out_ref, acc):
    slots, rows, _ = tile_ref.shape
    acc[...] = jnp.zeros_like(acc)
    for s in range(slots):

        @pl.when(s < meta_ref[step, s, 3])
        def _(s=s):
            block = jnp.concatenate([mine_ref[s], other_ref[s]], axis=0)
            got = lax.dot_general(
                tile_ref[s], block, (((1,), (1,)), ((), ())), preferred_element_type=jnp.float32
            )
            place = pl.ds(pl.multiple_of(meta_ref[step, s, 1] * TM, TM), TM)
            acc[meta_ref[step, s, 2], :, place, :] += got.reshape(rows // TM, TM, got.shape[1])

    out_ref[...] = acc[...].astype(out_ref.dtype)


def exchange_kernel(n_bas, n_aux, n_orb, where_ref, *refs):
    halves, keep_ref, send_ref, stack = refs[:n_bas], refs[n_bas], refs[n_bas + 1], refs[n_bas + 2]
    me, aux, orb = where_ref[0], where_ref[1], where_ref[2]
    pairs, per = halves[0].shape[1] // 2, halves[0].shape[0]
    for step in range(n_bas):
        stack[:, :, step] = halves[step][...]
    total = None
    for block in range(per):
        for pair in range(pairs):
            first, second = 2 * pair, 2 * pair + 1
            wide = jnp.concatenate(
                [
                    stack[block, first].reshape(n_bas * ROWS, -1),
                    stack[block, second].reshape(n_bas * ROWS, -1),
                ],
                axis=1,
            )
            tall = []
            for o in range(n_orb):
                for a in range(n_aux):
                    group = lax.rem(aux + a, n_aux) * n_orb + lax.rem(orb + o, n_orb)
                    back = lax.rem(me - group + n_bas * n_aux * n_orb, n_bas)
                    tall.append(
                        jnp.concatenate([stack[block, first, back], stack[block, second, back]], axis=1)
                    )
            got = lax.dot_general(
                jnp.concatenate(tall, axis=0),
                wide,
                (((1,), (1,)), ((), ())),
                preferred_element_type=jnp.float32,
            )
            total = got if total is None else total + got
    keep_ref[...] = total[: n_aux * ROWS].reshape(keep_ref.shape)
    send_ref[...] = total[n_aux * ROWS :].reshape(send_ref.shape)


def body(n_bas, n_aux, n_orb, tiles, screen, counts, orbitals):
    slots, rows, width = tiles.shape
    bas, aux, orb = lax.axis_index("bas"), lax.axis_index("aux"), lax.axis_index("orb")
    where = jnp.stack([bas, aux, orb]).astype(jnp.int32)
    coeff = orbitals.T
    count, basis = coeff.shape
    depth = count // 2
    params = pltpu.CompilerParams(vmem_limit_bytes=VMEM_LIMIT)

    half_rows = lax.dynamic_slice_in_dim(coeff, (aux % 2) * depth, depth, 0)
    pieces = []
    for step in range(1, n_bas):
        got = shift(half_rows, "bas", step, n_bas)
        pieces.append((got, swap(got, "aux", n_aux)))
    meta = jnp.concatenate([screen, jnp.broadcast_to(counts, (slots, 1))], axis=1)
    metas = jnp.stack([meta] + [shift(meta, "bas", step, n_bas) for step in range(1, n_bas)])

    part = rows // (n_bas * n_orb)

    def chunk(dest):
        return lax.dynamic_slice_in_dim(tiles, (dest * n_orb + orb) * part, part, 1)

    arrived = [chunk(bas)]
    for step in range(1, n_bas):
        arrived.append(shift(chunk((bas + step) % n_bas), "bas", step, n_bas))

    low = aux % 2 == 0
    ordered = [x for pair in pieces for x in pair]
    mine = pl.pallas_call(
        functools.partial(select_kernel, n_bas, basis // width),
        out_shape=jax.ShapeDtypeStruct((n_bas * slots, count, width), coeff.dtype),
        in_specs=[smem(), smem()] + [vmem()] * (1 + len(ordered)),
        out_specs=vmem(),
        compiler_params=params,
        name="select",
    )(where, metas, jnp.where(low, coeff, jnp.roll(coeff, depth, axis=0)), *ordered)
    other = swap(mine, "orb", n_orb)

    halves = []
    for step in range(n_bas):
        spec = pl.BlockSpec((slots, count, width), lambda g, step=step: (step, 0, 0))
        halves.append(
            pl.pallas_call(
                functools.partial(product_kernel, step),
                grid=(1,),
                out_shape=jax.ShapeDtypeStruct((PBLK, part // TM, ROWS, n_orb * count), jnp.bfloat16),
                in_specs=[smem(), vmem(), spec, spec],
                out_specs=vmem(),
                scratch_shapes=[pltpu.VMEM((PBLK, part // TM, ROWS, n_orb * count), jnp.float32)],
                compiler_params=params,
                name="product",
            )(metas, arrived[step], mine, other)
        )

    strip = jax.ShapeDtypeStruct((n_aux, ROWS, n_bas * ROWS), jnp.float32)
    keep, send = pl.pallas_call(
        functools.partial(exchange_kernel, n_bas, n_aux, n_orb),
        out_shape=(strip, strip),
        in_specs=[smem()] + [vmem()] * n_bas,
        out_specs=(vmem(), vmem()),
        scratch_shapes=[pltpu.VMEM((PBLK, part // TM, n_bas, ROWS, n_orb * count), jnp.bfloat16)],
        compiler_params=params,
        name="exchange",
    )(where, *halves)

    strips = keep + swap(send, "orb", n_orb)
    strip = strips[0]
    for step in range(1, n_aux):
        strip = strip + shift(strips[step], "aux", step, n_aux)
    total = strip[:, :ROWS]
    for step in range(1, n_bas):
        total = total + shift(strip[:, step * ROWS : (step + 1) * ROWS], "bas", -step, n_bas)
    return total.T


def solution(mesh):
    placed = (
        P(("frag", "bas", "aux"), None, None),
        P(("frag", "bas", "aux"), None),
        P(("frag", "bas", "aux"), None),
        P(("frag", "bas"), "orb"),
    )
    sizes = mesh.shape
    return jax.shard_map(
        functools.partial(body, sizes["bas"], sizes["aux"], sizes["orb"]),
        mesh=mesh,
        in_specs=placed,
        out_specs=P(("frag", "bas"), ("aux", "orb")),
        check_vma=False,
    )
```

```python
import functools

import jax
import jax.numpy as jnp
from jax import lax
from jax.experimental import pallas as pl
from jax.experimental.pallas import tpu as pltpu
from jax.sharding import PartitionSpec as P

PBLK = 2
TM = 8
MSUB = 8
ROWS = MSUB * TM
VMEM_LIMIT = 40 * 1024 * 1024


def swap(x, axis, size, step=1):
    return lax.ppermute(x, axis, [(i, i ^ step) for i in range(size)])


def after(x, *others):
    return lax.optimization_barrier((x, *others))[0]


def vmem():
    return pl.BlockSpec(memory_space=pltpu.VMEM)


def smem():
    return pl.BlockSpec(memory_space=pltpu.SMEM)


def select_kernel(n_bas, blocks, where_ref, meta_ref, *refs):
    pieces, out_refs, table = refs[:n_bas], refs[n_bas:-1], refs[-1]
    me, aux = where_ref[0], where_ref[1]
    count = table.shape[1]
    depth = count // 2
    slots = meta_ref.shape[2]
    for step in range(n_bas):
        if len(pieces[step]) == 1:
            table[step] = pieces[step][0][...]
        else:
            for side in range(2):
                start = pl.multiple_of(((aux + side) % 2) * depth, depth)
                table[step, pl.ds(start, depth), :] = pieces[step][side][:, : table.shape[2]]
    for source in range(n_bas):
        for s in range(slots):
            block = meta_ref[source, 0, s]
            owner = block // blocks
            lanes = pl.ds(pl.multiple_of((block - owner * blocks) * 128, 128), 128)
            out_refs[source][s] = table[me ^ owner, :, lanes]


def exchange_kernel(n_bas, n_aux, n_orb, where_ref, meta_ref, *refs):
    tiles, mine, other = refs[:n_bas], refs[n_bas : 2 * n_bas], refs[2 * n_bas : 3 * n_bas]
    keep_ref, send_ref, acc, total = refs[3 * n_bas :]
    me, aux, orb = where_ref[0], where_ref[1], where_ref[2]
    slots, rows, _ = tiles[0].shape
    turn = me ^ (aux * n_orb + orb)
    places = [((step ^ turn) % n_orb) * n_aux + (step ^ turn) // n_orb for step in range(n_bas)]
    acc[...] = jnp.zeros_like(acc)
    for step in range(n_bas):
        for s in range(slots):
            block = jnp.concatenate([mine[step][s], other[step][s]], axis=0)
            got = lax.dot_general(
                tiles[step][s], block, (((1,), (1,)), ((), ())), preferred_element_type=jnp.float32
            )
            got = jnp.where(meta_ref[step, 3, s] > s, got, 0.0)
            place = pl.ds(pl.multiple_of(meta_ref[step, 1, s] * TM, TM), TM)
            where = (meta_ref[step, 2, s], slice(None), places[step], place)
            acc[where] += got.reshape(rows // TM, TM, got.shape[1])
    sums = None
    for block in range(acc.shape[0]):
        for pair in range(acc.shape[1] // 2):
            wide = jnp.concatenate(
                [acc[block, 2 * pair + k].reshape(n_bas * ROWS, -1).astype(jnp.bfloat16) for k in range(2)],
                axis=1,
            )
            got = lax.dot_general(
                wide, wide, (((1,), (1,)), ((), ())), preferred_element_type=jnp.float32
            )
            sums = got if sums is None else sums + got
    total[...] = sums.reshape(total.shape)
    half = n_aux * ROWS
    for step in range(n_bas):
        keep_ref[step] = total[places[step], :, :half]
        send_ref[step] = total[places[step], :, half:]


def body(n_bas, n_aux, n_orb, tiles, screen, counts, orbitals):
    slots, rows, width = tiles.shape
    bas, aux, orb = lax.axis_index("bas"), lax.axis_index("aux"), lax.axis_index("orb")
    where = jnp.stack([bas, aux, orb]).astype(jnp.int32)
    coeff = orbitals.T
    count, basis = coeff.shape
    depth = count // 2
    params = pltpu.CompilerParams(vmem_limit_bytes=VMEM_LIMIT)

    meta = jnp.concatenate([screen.T, jnp.broadcast_to(counts, (1, slots))]).astype(coeff.dtype)
    label = jnp.pad(meta, ((0, depth - meta.shape[0]), (0, width - slots)))
    half_rows = lax.dynamic_slice_in_dim(coeff, (aux % 2) * depth, depth, 0)
    message = jnp.concatenate([half_rows, label], axis=1)
    firsts = [message] + [None] * (n_bas - 1)
    for step in sorted(range(1, n_bas), key=lambda step: step & (step - 1) != 0):
        top = 1 << (step.bit_length() - 1)
        low = step ^ top
        firsts[step] = (
            swap(firsts[top], "bas", n_bas, low) if low else swap(message, "bas", n_bas, top)
        )
    metas = [got[: meta.shape[0], basis : basis + slots].astype(jnp.int32) for got in firsts]

    part = rows // (n_bas * n_orb)

    def chunk(dest):
        return lax.dynamic_slice_in_dim(tiles, (dest * n_orb + orb) * part, part, 1)

    seconds = [None] + [swap(got, "aux", n_aux) for got in firsts[1:]]
    arrived = [chunk(bas)]
    for step in range(1, n_bas):
        gate = firsts[1] if step == n_bas // 2 else seconds[n_bas // 2]
        arrived.append(swap(after(chunk(bas ^ step), gate), "bas", n_bas, step))
    pieces = [[coeff]]
    for step in range(1, n_bas):
        pieces.append([firsts[step], seconds[step]])
    metas = jnp.stack(metas)

    def select(where_ref, meta_ref, *refs):
        groups, at = [], 0
        for piece in pieces:
            groups.append(refs[at : at + len(piece)])
            at += len(piece)
        select_kernel(n_bas, basis // width, where_ref, meta_ref, *groups, *refs[at:])

    flat = [x for piece in pieces for x in piece]
    mine = pl.pallas_call(
        select,
        out_shape=[jax.ShapeDtypeStruct((slots, count, width), coeff.dtype)] * n_bas,
        in_specs=[smem(), smem()] + [vmem()] * len(flat),
        out_specs=[vmem()] * n_bas,
        scratch_shapes=[pltpu.VMEM((n_bas, count, basis), coeff.dtype)],
        compiler_params=params,
        name="select",
    )(where, metas, *flat)
    other = [swap(part, "orb", n_orb) for part in mine]

    strip = jax.ShapeDtypeStruct((n_bas, ROWS, n_aux * ROWS), jnp.float32)
    keep, send = pl.pallas_call(
        functools.partial(exchange_kernel, n_bas, n_aux, n_orb),
        out_shape=(strip, strip),
        in_specs=[smem(), smem()] + [vmem()] * (3 * n_bas),
        out_specs=(vmem(), vmem()),
        scratch_shapes=[
            pltpu.VMEM((PBLK, part // TM, n_bas, ROWS, n_orb * count), jnp.float32),
            pltpu.VMEM((n_bas, ROWS, n_bas * ROWS), jnp.float32),
        ],
        compiler_params=params,
        name="exchange",
    )(where, metas, *arrived, *mine, *other)

    strip = keep + swap(send, "orb", n_orb)
    while strip.shape[0] > 1:
        step = strip.shape[0] // 2
        strip = strip[:step] + swap(strip[step:], "bas", n_bas, step)
    strip = strip[0]
    total = strip[:, :ROWS]
    for step in range(1, n_aux):
        total = total + swap(strip[:, step * ROWS : (step + 1) * ROWS], "aux", n_aux, step)
    return total


def solution(mesh):
    placed = (
        P(("frag", "bas", "aux"), None, None),
        P(("frag", "bas", "aux"), None),
        P(("frag", "bas", "aux"), None),
        P(("frag", "bas"), "orb"),
    )
    sizes = mesh.shape
    return jax.shard_map(
        functools.partial(body, sizes["bas"], sizes["aux"], sizes["orb"]),
        mesh=mesh,
        in_specs=placed,
        out_specs=P(("frag", "bas"), ("aux", "orb")),
        check_vma=False,
    )
```

```python
import functools

import jax
import jax.numpy as jnp
from jax import lax
from jax.experimental import pallas as pl
from jax.experimental.pallas import tpu as pltpu
from jax.sharding import PartitionSpec as P

PBLK = 2
TM = 8
MSUB = 8
ROWS = MSUB * TM
PIECES = 2
VMEM_LIMIT = 40 * 1024 * 1024


def swap(x, axis, size, step=1):
    return lax.ppermute(x, axis, [(i, i ^ step) for i in range(size)])


def after(x, *others):
    return lax.optimization_barrier((x, *others))[0]


def cut(total, pieces):
    return [total * (i + 1) // pieces - total * i // pieces for i in range(pieces)]


def spread(refs):
    return [(ref, i) for ref in refs for i in range(ref.shape[0])]


def vmem():
    return pl.BlockSpec(memory_space=pltpu.VMEM)


def smem():
    return pl.BlockSpec(memory_space=pltpu.SMEM)


def select_kernel(n_bas, blocks, where_ref, meta_ref, *refs):
    pieces, out_refs, table = refs[:n_bas], refs[n_bas:-1], refs[-1]
    me, aux = where_ref[0], where_ref[1]
    count = table.shape[1]
    depth = count // 2
    slots = meta_ref.shape[2]
    for step in range(n_bas):
        if len(pieces[step]) == 1:
            table[step] = pieces[step][0][...]
        else:
            for side in range(2):
                start = pl.multiple_of(((aux + side) % 2) * depth, depth)
                table[step, pl.ds(start, depth), :] = pieces[step][side][:, : table.shape[2]]
    places = spread(out_refs)
    for source in range(n_bas):
        for s in range(slots):
            block = meta_ref[source, 0, s]
            owner = block // blocks
            lanes = pl.ds(pl.multiple_of((block - owner * blocks) * 128, 128), 128)
            ref, at = places[source * slots + s]
            ref[at] = table[me ^ owner, :, lanes]


def exchange_kernel(n_bas, n_aux, n_orb, where_ref, meta_ref, *refs):
    tiles, mine, other = refs[:n_bas], spread(refs[n_bas : n_bas + PIECES]), spread(refs[n_bas + PIECES : n_bas + 2 * PIECES])
    keep_ref, send_ref, acc, total = refs[n_bas + 2 * PIECES :]
    me, aux, orb = where_ref[0], where_ref[1], where_ref[2]
    slots, rows, _ = tiles[0].shape
    turn = me ^ (aux * n_orb + orb)
    places = [((step ^ turn) % n_orb) * n_aux + (step ^ turn) // n_orb for step in range(n_bas)]
    acc[...] = jnp.zeros_like(acc)
    for step in range(n_bas):
        for s in range(slots):
            index = step * slots + s
            block = jnp.concatenate([ref[at] for ref, at in (mine[index], other[index])], axis=0)
            got = lax.dot_general(
                tiles[step][s], block, (((1,), (1,)), ((), ())), preferred_element_type=jnp.float32
            )
            got = jnp.where(meta_ref[step, 3, 0] > s, got, 0.0)
            place = pl.ds(pl.multiple_of(meta_ref[step, 1, s] * TM, TM), TM)
            where = (meta_ref[step, 2, s], slice(None), places[step], place)
            acc[where] += got.reshape(rows // TM, TM, got.shape[1])
    sums = None
    for block in range(acc.shape[0]):
        for pair in range(acc.shape[1] // 2):
            wide = jnp.concatenate(
                [acc[block, 2 * pair + k].reshape(n_bas * ROWS, -1).astype(jnp.bfloat16) for k in range(2)],
                axis=1,
            )
            got = lax.dot_general(
                wide, wide, (((1,), (1,)), ((), ())), preferred_element_type=jnp.float32
            )
            sums = got if sums is None else sums + got
    total[...] = sums.reshape(total.shape)
    half = n_aux * ROWS
    for step in range(n_bas):
        keep_ref[step] = total[places[step], :, :half]
        send_ref[step] = total[places[step], :, half:]


def body(n_bas, n_aux, n_orb, tiles, screen, counts, orbitals):
    slots, rows, width = tiles.shape
    bas, aux, orb = lax.axis_index("bas"), lax.axis_index("aux"), lax.axis_index("orb")
    where = jnp.stack([bas, aux, orb]).astype(jnp.int32)
    coeff = orbitals.T
    count, basis = coeff.shape
    depth = count // 2
    params = pltpu.CompilerParams(vmem_limit_bytes=VMEM_LIMIT)

    meta = jnp.concatenate([screen.T, jnp.pad(counts, ((0, 0), (0, slots - 1)))]).astype(coeff.dtype)
    label = jnp.pad(meta, ((0, depth - meta.shape[0]), (0, width - slots)))
    half_rows = lax.dynamic_slice_in_dim(coeff, (aux % 2) * depth, depth, 0)
    message = jnp.concatenate([half_rows, label], axis=1)
    firsts = [message] + [None] * (n_bas - 1)
    for step in sorted(range(1, n_bas), key=lambda step: step & (step - 1) != 0):
        top = 1 << (step.bit_length() - 1)
        low = step ^ top
        firsts[step] = (
            swap(firsts[top], "bas", n_bas, low) if low else swap(message, "bas", n_bas, top)
        )
    metas = [got[: meta.shape[0], basis : basis + slots].astype(jnp.int32) for got in firsts]

    part = rows // (n_bas * n_orb)

    def chunk(dest):
        return lax.dynamic_slice_in_dim(tiles, (dest * n_orb + orb) * part, part, 1)

    seconds = [None, swap(firsts[1], "aux", n_aux)]
    for step in range(2, n_bas):
        seconds.append(swap(after(firsts[step], seconds[-1]), "aux", n_aux))
    arrived = [chunk(bas)]
    for step in range(1, n_bas):
        gate = firsts[1] if step == n_bas // 2 else seconds[1]
        arrived.append(swap(after(chunk(bas ^ step), gate), "bas", n_bas, step))
    pieces = [[coeff]]
    for step in range(1, n_bas):
        pieces.append([firsts[step], seconds[step]])
    metas = jnp.stack(metas)

    def select(where_ref, meta_ref, *refs):
        groups, at = [], 0
        for piece in pieces:
            groups.append(refs[at : at + len(piece)])
            at += len(piece)
        select_kernel(n_bas, basis // width, where_ref, meta_ref, *groups, *refs[at:])

    flat = [x for piece in pieces for x in piece]
    sizes = cut(n_bas * slots, PIECES)
    mine = pl.pallas_call(
        select,
        out_shape=[jax.ShapeDtypeStruct((size, count, width), coeff.dtype) for size in sizes],
        in_specs=[smem(), smem()] + [vmem()] * len(flat),
        out_specs=[vmem()] * len(sizes),
        scratch_shapes=[pltpu.VMEM((n_bas, count, basis), coeff.dtype)],
        compiler_params=params,
        name="select",
    )(where, metas, *flat)
    other = [swap(part, "orb", n_orb) for part in mine]

    strip = jax.ShapeDtypeStruct((n_bas, ROWS, n_aux * ROWS), jnp.float32)
    keep, send = pl.pallas_call(
        functools.partial(exchange_kernel, n_bas, n_aux, n_orb),
        out_shape=(strip, strip),
        in_specs=[smem(), smem()] + [vmem()] * (n_bas + 2 * PIECES),
        out_specs=(vmem(), vmem()),
        scratch_shapes=[
            pltpu.VMEM((PBLK, part // TM, n_bas, ROWS, n_orb * count), jnp.float32),
            pltpu.VMEM((n_bas, ROWS, n_bas * ROWS), jnp.float32),
        ],
        compiler_params=params,
        name="exchange",
    )(where, metas, *arrived, *mine, *other)

    strips = keep + swap(send, "orb", n_orb)
    strip = strips[0]
    for step in range(1, n_bas):
        strip = strip + swap(strips[step], "bas", n_bas, step)
    total = strip[:, :ROWS]
    for step in range(1, n_aux):
        total = total + swap(strip[:, step * ROWS : (step + 1) * ROWS], "aux", n_aux, step)
    return total


def solution(mesh):
    placed = (
        P(("frag", "bas", "aux"), None, None),
        P(("frag", "bas", "aux"), None),
        P(("frag", "bas", "aux"), None),
        P(("frag", "bas"), "orb"),
    )
    sizes = mesh.shape
    return jax.shard_map(
        functools.partial(body, sizes["bas"], sizes["aux"], sizes["orb"]),
        mesh=mesh,
        in_specs=placed,
        out_specs=P(("frag", "bas"), ("aux", "orb")),
        check_vma=False,
    )
```

```python
import functools

import jax
import jax.numpy as jnp
from jax import lax
from jax.experimental import pallas as pl
from jax.experimental.pallas import tpu as pltpu
from jax.sharding import PartitionSpec as P

PBLK = 2
TM = 8
MSUB = 8
ROWS = MSUB * TM
PIECES = 2
VMEM_LIMIT = 40 * 1024 * 1024


def swap(x, axis, size, step=1):
    return lax.ppermute(x, axis, [(i, i ^ step) for i in range(size)])


def after(x, *others):
    return lax.optimization_barrier((x, *others))[0]


def cut(total, pieces):
    return [total * (i + 1) // pieces - total * i // pieces for i in range(pieces)]


def spread(refs):
    return [(ref, i) for ref in refs for i in range(ref.shape[0])]


def vmem():
    return pl.BlockSpec(memory_space=pltpu.VMEM)


def smem():
    return pl.BlockSpec(memory_space=pltpu.SMEM)


def select_kernel(n_bas, blocks, where_ref, meta_ref, *refs):
    pieces, out_refs, table = refs[:n_bas], refs[n_bas:-1], refs[-1]
    me, aux = where_ref[0], where_ref[1]
    count = table.shape[1]
    depth = count // 2
    slots = meta_ref.shape[2]
    for step in range(n_bas):
        if len(pieces[step]) == 1:
            table[step] = pieces[step][0][...]
        else:
            for side in range(2):
                start = pl.multiple_of(((aux + side) % 2) * depth, depth)
                table[step, pl.ds(start, depth), :] = pieces[step][side][:, : table.shape[2]]
    places = spread(out_refs)
    for source in range(n_bas):
        for s in range(slots):
            block = meta_ref[source, 0, s]
            owner = block // blocks
            lanes = pl.ds(pl.multiple_of((block - owner * blocks) * 128, 128), 128)
            ref, at = places[source * slots + s]
            ref[at] = table[me ^ owner, :, lanes]


def exchange_kernel(n_bas, n_aux, n_orb, where_ref, meta_ref, *refs):
    tiles, refs = refs[:n_bas], refs[n_bas:]
    mine, other = spread(refs[:PIECES]), spread(refs[PIECES : 2 * PIECES])
    keep_ref, send_ref, acc, total = refs[2 * PIECES :]
    me, aux, orb = where_ref[0], where_ref[1], where_ref[2]
    slots, rows, _ = tiles[0].shape
    turn = me ^ (aux * n_orb + orb)
    places = [((step ^ turn) % n_orb) * n_aux + (step ^ turn) // n_orb for step in range(n_bas)]
    acc[...] = jnp.zeros_like(acc)
    for step in range(n_bas):
        for s in range(slots):
            index = step * slots + s
            block = jnp.concatenate([ref[at] for ref, at in (mine[index], other[index])], axis=0)
            got = lax.dot_general(
                tiles[step][s], block, (((1,), (1,)), ((), ())), preferred_element_type=jnp.float32
            )
            place = pl.ds(pl.multiple_of(meta_ref[step, 1, s] * TM, TM), TM)
            where = (meta_ref[step, 2, s], slice(None), places[step], place)
            acc[where] += got.reshape(rows // TM, TM, got.shape[1])
    sums = None
    for block in range(acc.shape[0]):
        for pair in range(acc.shape[1] // 2):
            wide = jnp.concatenate(
                [acc[block, 2 * pair + k].reshape(n_bas * ROWS, -1).astype(jnp.bfloat16) for k in range(2)],
                axis=1,
            )
            got = lax.dot_general(
                wide, wide, (((1,), (1,)), ((), ())), preferred_element_type=jnp.float32
            )
            sums = got if sums is None else sums + got
    total[...] = sums.reshape(total.shape)
    half = n_aux * ROWS
    for step in range(n_bas):
        keep_ref[step] = total[places[step], :, :half]
        send_ref[step] = total[places[step], :, half:]


def body(n_bas, n_aux, n_orb, tiles, screen, counts, orbitals):
    slots, rows, width = tiles.shape
    bas, aux, orb = lax.axis_index("bas"), lax.axis_index("aux"), lax.axis_index("orb")
    where = jnp.stack([bas, aux, orb]).astype(jnp.int32)
    coeff = orbitals.T
    count, basis = coeff.shape
    depth = count // 2
    params = pltpu.CompilerParams(vmem_limit_bytes=VMEM_LIMIT)

    meta = screen.T.astype(coeff.dtype)
    label = jnp.pad(meta, ((0, depth - meta.shape[0]), (0, width - slots)))
    half_rows = lax.dynamic_slice_in_dim(coeff, (aux % 2) * depth, depth, 0)
    message = jnp.concatenate([half_rows, label], axis=1)
    firsts = [message] + [None] * (n_bas - 1)
    for step in sorted(range(1, n_bas), key=lambda step: step & (step - 1) != 0):
        top = 1 << (step.bit_length() - 1)
        low = step ^ top
        firsts[step] = (
            swap(firsts[top], "bas", n_bas, low) if low else swap(message, "bas", n_bas, top)
        )
    metas = [got[: meta.shape[0], basis : basis + slots].astype(jnp.int32) for got in firsts]

    part = rows // (n_bas * n_orb)
    live = jnp.arange(slots) < after(counts, message)[0, 0]

    def chunk(dest):
        taken = lax.dynamic_slice_in_dim(tiles, (dest * n_orb + orb) * part, part, 1)
        return jnp.where(live[:, None, None], taken, 0)

    seconds = [None, swap(firsts[1], "aux", n_aux)]
    for step in range(2, n_bas):
        seconds.append(swap(after(firsts[step], seconds[-1]), "aux", n_aux))
    arrived = [chunk(bas)]
    for step in range(1, n_bas):
        gate = firsts[1] if step == n_bas // 2 else seconds[1]
        arrived.append(swap(after(chunk(bas ^ step), gate), "bas", n_bas, step))
    pieces = [[coeff]]
    for step in range(1, n_bas):
        pieces.append([firsts[step], seconds[step]])
    metas = jnp.stack(metas)

    def select(where_ref, meta_ref, *refs):
        groups, at = [], 0
        for piece in pieces:
            groups.append(refs[at : at + len(piece)])
            at += len(piece)
        select_kernel(n_bas, basis // width, where_ref, meta_ref, *groups, *refs[at:])

    flat = [x for piece in pieces for x in piece]
    sizes = cut(n_bas * slots, PIECES)
    mine = pl.pallas_call(
        select,
        out_shape=[jax.ShapeDtypeStruct((size, count, width), coeff.dtype) for size in sizes],
        in_specs=[smem(), smem()] + [vmem()] * len(flat),
        out_specs=[vmem()] * len(sizes),
        scratch_shapes=[pltpu.VMEM((n_bas, count, basis), coeff.dtype)],
        compiler_params=params,
        name="select",
    )(where, metas, *flat)
    other = [swap(part, "orb", n_orb) for part in mine]

    strip = jax.ShapeDtypeStruct((n_bas, ROWS, n_aux * ROWS), jnp.float32)
    keep, send = pl.pallas_call(
        functools.partial(exchange_kernel, n_bas, n_aux, n_orb),
        out_shape=(strip, strip),
        in_specs=[smem(), smem()] + [vmem()] * (n_bas + 2 * PIECES),
        out_specs=(vmem(), vmem()),
        scratch_shapes=[
            pltpu.VMEM((PBLK, part // TM, n_bas, ROWS, n_orb * count), jnp.float32),
            pltpu.VMEM((n_bas, ROWS, n_bas * ROWS), jnp.float32),
        ],
        compiler_params=params,
        name="exchange",
    )(where, metas, *arrived, *mine, *other)

    strips = keep + swap(send, "orb", n_orb)
    strip = strips[0]
    for step in range(1, n_bas):
        strip = strip + swap(strips[step], "bas", n_bas, step)
    total = strip[:, :ROWS]
    for step in range(1, n_aux):
        total = total + swap(strip[:, step * ROWS : (step + 1) * ROWS], "aux", n_aux, step)
    return total


def solution(mesh):
    placed = (
        P(("frag", "bas", "aux"), None, None),
        P(("frag", "bas", "aux"), None),
        P(("frag", "bas", "aux"), None),
        P(("frag", "bas"), "orb"),
    )
    sizes = mesh.shape
    return jax.shard_map(
        functools.partial(body, sizes["bas"], sizes["aux"], sizes["orb"]),
        mesh=mesh,
        in_specs=placed,
        out_specs=P(("frag", "bas"), ("aux", "orb")),
        check_vma=False,
    )
```

```python
import functools

import jax
import jax.numpy as jnp
from jax import lax
from jax.experimental import pallas as pl
from jax.experimental.pallas import tpu as pltpu
from jax.sharding import PartitionSpec as P

PBLK = 2
TM = 8
MSUB = 8
ROWS = MSUB * TM
PIECES = 2
VMEM_LIMIT = 40 * 1024 * 1024


def swap(x, axis, size, step=1):
    return lax.ppermute(x, axis, [(i, i ^ step) for i in range(size)])


def after(x, *others):
    return lax.optimization_barrier((x, *others))[0]


def cut(total, pieces):
    return [total * (i + 1) // pieces - total * i // pieces for i in range(pieces)]


def spread(refs):
    return [(ref, i) for ref in refs for i in range(ref.shape[0])]


def vmem():
    return pl.BlockSpec(memory_space=pltpu.VMEM)


def smem():
    return pl.BlockSpec(memory_space=pltpu.SMEM)


def select_kernel(n_bas, blocks, where_ref, meta_ref, *refs):
    pieces, out_refs, table = refs[:n_bas], refs[n_bas:-1], refs[-1]
    me, aux = where_ref[0], where_ref[1]
    count = table.shape[1]
    depth = count // 2
    slots = meta_ref.shape[2]
    for step in range(n_bas):
        if len(pieces[step]) == 1:
            table[step] = pieces[step][0][...]
        else:
            for side in range(2):
                start = pl.multiple_of(((aux + side) % 2) * depth, depth)
                table[step, pl.ds(start, depth), :] = pieces[step][side][:, : table.shape[2]]
    places = spread(out_refs)
    for source in range(n_bas):
        for s in range(slots):
            block = meta_ref[source, 0, s]
            owner = block // blocks
            lanes = pl.ds(pl.multiple_of((block - owner * blocks) * 128, 128), 128)
            ref, at = places[source * slots + s]
            ref[at] = table[me ^ owner, :, lanes]


def exchange_kernel(n_bas, n_aux, n_orb, where_ref, meta_ref, *refs):
    tiles, refs = refs[:n_bas], refs[n_bas:]
    mine, other = spread(refs[:PIECES]), spread(refs[PIECES : 2 * PIECES])
    keep_ref, send_ref, acc, total = refs[2 * PIECES :]
    me, aux, orb = where_ref[0], where_ref[1], where_ref[2]
    slots, rows, _ = tiles[0].shape
    turn = me ^ (aux * n_orb + orb)
    places = [((step ^ turn) % n_orb) * n_aux + (step ^ turn) // n_orb for step in range(n_bas)]
    acc[...] = jnp.zeros_like(acc)
    for step in range(n_bas):
        for s in range(slots):
            index = step * slots + s
            block = jnp.concatenate([ref[at] for ref, at in (mine[index], other[index])], axis=0)
            got = lax.dot_general(
                tiles[step][s], block, (((1,), (1,)), ((), ())), preferred_element_type=jnp.float32
            )
            place = pl.ds(pl.multiple_of(meta_ref[step, 1, s] * TM, TM), TM)
            where = (meta_ref[step, 2, s], slice(None), places[step], place)
            acc[where] += got.reshape(rows // TM, TM, got.shape[1])
    sums = None
    for block in range(acc.shape[0]):
        for pair in range(acc.shape[1] // 2):
            wide = jnp.concatenate(
                [acc[block, 2 * pair + k].reshape(n_bas * ROWS, -1).astype(jnp.bfloat16) for k in range(2)],
                axis=1,
            )
            got = lax.dot_general(
                wide, wide, (((1,), (1,)), ((), ())), preferred_element_type=jnp.float32
            )
            sums = got if sums is None else sums + got
    total[...] = sums.reshape(total.shape)
    half = n_aux * ROWS
    for step in range(n_bas):
        keep_ref[step] = total[places[step], :, :half]
        send_ref[step] = total[places[step], :, half:]


def body(n_bas, n_aux, n_orb, tiles, screen, counts, orbitals):
    slots, rows, width = tiles.shape
    bas, aux, orb = lax.axis_index("bas"), lax.axis_index("aux"), lax.axis_index("orb")
    where = jnp.stack([bas, aux, orb]).astype(jnp.int32)
    coeff = orbitals.T
    count, basis = coeff.shape
    depth = count // 2
    params = pltpu.CompilerParams(vmem_limit_bytes=VMEM_LIMIT)

    meta = screen.T.astype(coeff.dtype)
    label = jnp.pad(meta, ((0, depth - meta.shape[0]), (0, width - slots)))
    half_rows = lax.dynamic_slice_in_dim(coeff, (aux % 2) * depth, depth, 0)
    message = jnp.concatenate([half_rows, label], axis=1)
    firsts = [message] + [None] * (n_bas - 1)
    for step in sorted(range(1, n_bas), key=lambda step: step & (step - 1) != 0):
        top = 1 << (step.bit_length() - 1)
        low = step ^ top
        firsts[step] = (
            swap(firsts[top], "bas", n_bas, low) if low else swap(message, "bas", n_bas, top)
        )
    metas = [got[: meta.shape[0], basis : basis + slots].astype(jnp.int32) for got in firsts]

    part = rows // (n_bas * n_orb)
    live = jnp.arange(slots) < after(counts, message)[0, 0]

    def chunk(dest):
        taken = lax.dynamic_slice_in_dim(tiles, (dest * n_orb + orb) * part, part, 1)
        return jnp.where(live[:, None, None], taken, 0)

    seconds = [None, swap(firsts[1], "aux", n_aux)]
    for step in range(2, n_bas):
        seconds.append(swap(after(firsts[step], seconds[-1]), "aux", n_aux))
    arrived = [chunk(bas)]
    for step in range(1, n_bas):
        gate = firsts[1] if step == n_bas // 2 else seconds[1]
        arrived.append(swap(after(chunk(bas ^ step), gate), "bas", n_bas, step))
    pieces = [[coeff]]
    for step in range(1, n_bas):
        pieces.append([firsts[step], seconds[step]])
    metas = jnp.stack(metas)

    def select(where_ref, meta_ref, *refs):
        groups, at = [], 0
        for piece in pieces:
            groups.append(refs[at : at + len(piece)])
            at += len(piece)
        select_kernel(n_bas, basis // width, where_ref, meta_ref, *groups, *refs[at:])

    flat = [x for piece in pieces for x in piece]
    sizes = cut(n_bas * slots, PIECES)
    mine = pl.pallas_call(
        select,
        out_shape=[jax.ShapeDtypeStruct((size, count, width), coeff.dtype) for size in sizes],
        in_specs=[smem(), smem()] + [vmem()] * len(flat),
        out_specs=[vmem()] * len(sizes),
        scratch_shapes=[pltpu.VMEM((n_bas, count, basis), coeff.dtype)],
        compiler_params=params,
        name="select",
    )(where, metas, *flat)
    other = [swap(part, "orb", n_orb) for part in mine]

    strip = jax.ShapeDtypeStruct((n_bas, ROWS, n_aux * ROWS), jnp.float32)
    keep, send = pl.pallas_call(
        functools.partial(exchange_kernel, n_bas, n_aux, n_orb),
        out_shape=(strip, strip),
        in_specs=[smem(), smem()] + [vmem()] * (n_bas + 2 * PIECES),
        out_specs=(vmem(), vmem()),
        scratch_shapes=[
            pltpu.VMEM((PBLK, part // TM, n_bas, ROWS, n_orb * count), jnp.float32),
            pltpu.VMEM((n_bas, ROWS, n_bas * ROWS), jnp.float32),
        ],
        compiler_params=params,
        name="exchange",
    )(where, metas, *arrived, *mine, *other)

    strips = keep + swap(send, "orb", n_orb)
    strip = strips[0]
    for step in sorted(range(1, n_bas), key=lambda step: step != n_bas // 2):
        strip = strip + swap(strips[step], "bas", n_bas, step)
    total = strip[:, :ROWS]
    for step in range(1, n_aux):
        total = total + swap(strip[:, step * ROWS : (step + 1) * ROWS], "aux", n_aux, step)
    return total


def solution(mesh):
    placed = (
        P(("frag", "bas", "aux"), None, None),
        P(("frag", "bas", "aux"), None),
        P(("frag", "bas", "aux"), None),
        P(("frag", "bas"), "orb"),
    )
    sizes = mesh.shape
    return jax.shard_map(
        functools.partial(body, sizes["bas"], sizes["aux"], sizes["orb"]),
        mesh=mesh,
        in_specs=placed,
        out_specs=P(("frag", "bas"), ("aux", "orb")),
        check_vma=False,
    )
```

```python
import functools

import jax
import jax.numpy as jnp
from jax import lax
from jax.experimental import pallas as pl
from jax.experimental.pallas import tpu as pltpu
from jax.sharding import PartitionSpec as P

PBLK = 2
TM = 8
MSUB = 8
ROWS = MSUB * TM
PIECES = 2
VMEM_LIMIT = 40 * 1024 * 1024


def swap(x, axis, size, step=1):
    return lax.ppermute(x, axis, [(i, i ^ step) for i in range(size)])


def after(x, *others):
    return lax.optimization_barrier((x, *others))[0]


def cut(total, pieces):
    return [total * (i + 1) // pieces - total * i // pieces for i in range(pieces)]


def spread(refs):
    return [(ref, i) for ref in refs for i in range(ref.shape[0])]


def vmem():
    return pl.BlockSpec(memory_space=pltpu.VMEM)


def smem():
    return pl.BlockSpec(memory_space=pltpu.SMEM)


def select_kernel(n_bas, blocks, where_ref, meta_ref, *refs):
    pieces, out_refs, table = refs[:n_bas], refs[n_bas:-1], refs[-1]
    me, aux = where_ref[0], where_ref[1]
    count = table.shape[1]
    depth = count // 2
    slots = meta_ref.shape[2]
    for step in range(n_bas):
        if len(pieces[step]) == 1:
            table[step] = pieces[step][0][...]
        else:
            for side in range(2):
                start = pl.multiple_of(((aux + side) % 2) * depth, depth)
                table[step, pl.ds(start, depth), :] = pieces[step][side][:, : table.shape[2]]
    places = spread(out_refs)
    for source in range(n_bas):
        for s in range(slots):
            block = meta_ref[source, 0, s]
            owner = block // blocks
            lanes = pl.ds(pl.multiple_of((block - owner * blocks) * 128, 128), 128)
            ref, at = places[source * slots + s]
            ref[at] = table[me ^ owner, :, lanes]


def exchange_kernel(n_bas, n_aux, n_orb, where_ref, meta_ref, *refs):
    tiles, refs = refs[:n_bas], refs[n_bas:]
    mine, other = spread(refs[:PIECES]), spread(refs[PIECES : 2 * PIECES])
    keep_ref, send_ref, acc, total = refs[2 * PIECES :]
    me, aux, orb = where_ref[0], where_ref[1], where_ref[2]
    slots, rows, _ = tiles[0].shape
    turn = me ^ (aux * n_orb + orb)
    places = [((step ^ turn) % n_orb) * n_aux + (step ^ turn) // n_orb for step in range(n_bas)]
    acc[...] = jnp.zeros_like(acc)
    for step in range(n_bas):
        for s in range(slots):
            index = step * slots + s
            block = jnp.concatenate([ref[at] for ref, at in (mine[index], other[index])], axis=0)
            got = lax.dot_general(
                tiles[step][s], block, (((1,), (1,)), ((), ())), preferred_element_type=jnp.float32
            )
            place = pl.ds(pl.multiple_of(meta_ref[step, 1, s] * TM, TM), TM)
            where = (meta_ref[step, 2, s], slice(None), places[step], place)
            acc[where] += got.reshape(rows // TM, TM, got.shape[1])
    sums = None
    for block in range(acc.shape[0]):
        for pair in range(acc.shape[1] // 2):
            wide = jnp.concatenate(
                [acc[block, 2 * pair + k].reshape(n_bas * ROWS, -1).astype(jnp.bfloat16) for k in range(2)],
                axis=1,
            )
            got = lax.dot_general(
                wide, wide, (((1,), (1,)), ((), ())), preferred_element_type=jnp.float32
            )
            sums = got if sums is None else sums + got
    total[...] = sums.reshape(total.shape)
    half = n_aux * ROWS
    for step in range(n_bas):
        keep_ref[step] = total[places[step], :, :half]
        send_ref[step] = total[places[step], :, half:]


def body(n_bas, n_aux, n_orb, tiles, screen, counts, orbitals):
    slots, rows, width = tiles.shape
    bas, aux, orb = lax.axis_index("bas"), lax.axis_index("aux"), lax.axis_index("orb")
    where = jnp.stack([bas, aux, orb]).astype(jnp.int32)
    coeff = orbitals.T
    count, basis = coeff.shape
    depth = count // 2
    params = pltpu.CompilerParams(vmem_limit_bytes=VMEM_LIMIT)

    meta = screen.T.astype(coeff.dtype)
    label = jnp.pad(meta, ((0, depth - meta.shape[0]), (0, width - slots)))
    half_rows = lax.dynamic_slice_in_dim(coeff, (aux % 2) * depth, depth, 0)
    message = jnp.concatenate([half_rows, label], axis=1)
    firsts = [message] + [None] * (n_bas - 1)
    for step in sorted(range(1, n_bas), key=lambda step: step & (step - 1) != 0):
        top = 1 << (step.bit_length() - 1)
        low = step ^ top
        firsts[step] = (
            swap(firsts[top], "bas", n_bas, low) if low else swap(message, "bas", n_bas, top)
        )
    metas = [got[: meta.shape[0], basis : basis + slots].astype(jnp.int32) for got in firsts]

    part = rows // (n_bas * n_orb)
    live = jnp.arange(slots) < after(counts, message)[0, 0]

    def chunk(dest):
        taken = lax.dynamic_slice_in_dim(tiles, (dest * n_orb + orb) * part, part, 1)
        return jnp.where(live[:, None, None], taken, 0)

    seconds = [None, swap(firsts[1], "aux", n_aux)]
    for step in range(2, n_bas):
        seconds.append(swap(after(firsts[step], seconds[-1]), "aux", n_aux))
    arrived = [chunk(bas)]
    for step in range(1, n_bas):
        gate = firsts[1] if step == n_bas // 2 else seconds[1]
        arrived.append(swap(after(chunk(bas ^ step), gate), "bas", n_bas, step))
    pieces = [[coeff]]
    for step in range(1, n_bas):
        pieces.append([firsts[step], seconds[step]])
    metas = jnp.stack(metas)

    def select(where_ref, meta_ref, *refs):
        groups, at = [], 0
        for piece in pieces:
            groups.append(refs[at : at + len(piece)])
            at += len(piece)
        select_kernel(n_bas, basis // width, where_ref, meta_ref, *groups, *refs[at:])

    flat = [x for piece in pieces for x in piece]
    sizes = cut(n_bas * slots, PIECES)
    mine = pl.pallas_call(
        select,
        out_shape=[jax.ShapeDtypeStruct((size, count, width), coeff.dtype) for size in sizes],
        in_specs=[smem(), smem()] + [vmem()] * len(flat),
        out_specs=[vmem()] * len(sizes),
        scratch_shapes=[pltpu.VMEM((n_bas, count, basis), coeff.dtype)],
        compiler_params=params,
        name="select",
    )(where, metas, *flat)
    other = [swap(part, "orb", n_orb) for part in mine]

    strip = jax.ShapeDtypeStruct((n_bas, ROWS, n_aux * ROWS), jnp.float32)
    keep, send = pl.pallas_call(
        functools.partial(exchange_kernel, n_bas, n_aux, n_orb),
        out_shape=(strip, strip),
        in_specs=[smem(), smem()] + [vmem()] * (n_bas + 2 * PIECES),
        out_specs=(vmem(), vmem()),
        scratch_shapes=[
            pltpu.VMEM((PBLK, part // TM, n_bas, ROWS, n_orb * count), jnp.float32),
            pltpu.VMEM((n_bas, ROWS, n_bas * ROWS), jnp.float32),
        ],
        compiler_params=params,
        name="exchange",
    )(where, metas, *arrived, *mine, *other)

    rest = keep[1:] + swap(send[1:], "orb", n_orb)
    strips = [keep[0] + swap(send[0], "orb", n_orb), *rest]
    strip = strips[0]
    for step in sorted(range(1, n_bas), key=lambda step: step != n_bas // 2):
        strip = strip + swap(strips[step], "bas", n_bas, step)
    total = strip[:, :ROWS]
    for step in range(1, n_aux):
        total = total + swap(strip[:, step * ROWS : (step + 1) * ROWS], "aux", n_aux, step)
    return total


def solution(mesh):
    placed = (
        P(("frag", "bas", "aux"), None, None),
        P(("frag", "bas", "aux"), None),
        P(("frag", "bas", "aux"), None),
        P(("frag", "bas"), "orb"),
    )
    sizes = mesh.shape
    return jax.shard_map(
        functools.partial(body, sizes["bas"], sizes["aux"], sizes["orb"]),
        mesh=mesh,
        in_specs=placed,
        out_specs=P(("frag", "bas"), ("aux", "orb")),
        check_vma=False,
    )
```

```python
import functools

import jax
import jax.numpy as jnp
from jax import lax
from jax.experimental import pallas as pl
from jax.experimental.pallas import tpu as pltpu
from jax.sharding import PartitionSpec as P

PBLK = 2
TM = 8
MSUB = 8
ROWS = MSUB * TM
PIECES = 3
VMEM_LIMIT = 40 * 1024 * 1024


def swap(x, axis, size, step=1):
    return lax.ppermute(x, axis, [(i, i ^ step) for i in range(size)])


def after(x, *others):
    return lax.optimization_barrier((x, *others))[0]


def cut(total, pieces):
    return [total * (i + 1) // pieces - total * i // pieces for i in range(pieces)]


def spread(refs):
    return [(ref, i) for ref in refs for i in range(ref.shape[0])]


def vmem():
    return pl.BlockSpec(memory_space=pltpu.VMEM)


def smem():
    return pl.BlockSpec(memory_space=pltpu.SMEM)


def select_kernel(n_bas, blocks, where_ref, meta_ref, *refs):
    pieces, out_refs, table = refs[:n_bas], refs[n_bas:-1], refs[-1]
    me, aux = where_ref[0], where_ref[1]
    count = table.shape[1]
    depth = count // 2
    slots = meta_ref.shape[2]
    for step in range(n_bas):
        if len(pieces[step]) == 1:
            table[step] = pieces[step][0][...]
        else:
            for side in range(2):
                start = pl.multiple_of(((aux + side) % 2) * depth, depth)
                table[step, pl.ds(start, depth), :] = pieces[step][side][:, : table.shape[2]]
    places = spread(out_refs)
    for source in range(n_bas):
        for s in range(slots):
            block = meta_ref[source, 0, s]
            owner = block // blocks
            lanes = pl.ds(pl.multiple_of((block - owner * blocks) * 128, 128), 128)
            ref, at = places[source * slots + s]
            ref[at] = table[me ^ owner, :, lanes]


def exchange_kernel(n_bas, n_aux, n_orb, where_ref, meta_ref, *refs):
    tiles, refs = refs[:n_bas], refs[n_bas:]
    mine, other = spread(refs[:PIECES]), spread(refs[PIECES : 2 * PIECES])
    keep_ref, send_ref, acc, total = refs[2 * PIECES :]
    me, aux, orb = where_ref[0], where_ref[1], where_ref[2]
    slots, rows, _ = tiles[0].shape
    turn = me ^ (aux * n_orb + orb)
    places = [((step ^ turn) % n_orb) * n_aux + (step ^ turn) // n_orb for step in range(n_bas)]
    acc[...] = jnp.zeros_like(acc)
    for step in range(n_bas):
        for s in range(slots):
            index = step * slots + s
            block = jnp.concatenate([ref[at] for ref, at in (mine[index], other[index])], axis=0)
            got = lax.dot_general(
                tiles[step][s], block, (((1,), (1,)), ((), ())), preferred_element_type=jnp.float32
            )
            place = pl.ds(pl.multiple_of(meta_ref[step, 1, s] * TM, TM), TM)
            where = (meta_ref[step, 2, s], slice(None), places[step], place)
            acc[where] += got.reshape(rows // TM, TM, got.shape[1])
    sums = None
    for block in range(acc.shape[0]):
        for pair in range(acc.shape[1] // 2):
            wide = jnp.concatenate(
                [acc[block, 2 * pair + k].reshape(n_bas * ROWS, -1).astype(jnp.bfloat16) for k in range(2)],
                axis=1,
            )
            got = lax.dot_general(
                wide, wide, (((1,), (1,)), ((), ())), preferred_element_type=jnp.float32
            )
            sums = got if sums is None else sums + got
    total[...] = sums.reshape(total.shape)
    half = n_aux * ROWS
    for step in range(n_bas):
        keep_ref[step] = total[places[step], :, :half]
        send_ref[step] = total[places[step], :, half:]


def body(n_bas, n_aux, n_orb, tiles, screen, counts, orbitals):
    slots, rows, width = tiles.shape
    bas, aux, orb = lax.axis_index("bas"), lax.axis_index("aux"), lax.axis_index("orb")
    where = jnp.stack([bas, aux, orb]).astype(jnp.int32)
    coeff = orbitals.T
    count, basis = coeff.shape
    depth = count // 2
    params = pltpu.CompilerParams(vmem_limit_bytes=VMEM_LIMIT)

    meta = screen.T.astype(coeff.dtype)
    label = jnp.pad(meta, ((0, depth - meta.shape[0]), (0, width - slots)))
    half_rows = lax.dynamic_slice_in_dim(coeff, (aux % 2) * depth, depth, 0)
    message = jnp.concatenate([half_rows, label], axis=1)
    firsts = [message] + [None] * (n_bas - 1)
    for step in sorted(range(1, n_bas), key=lambda step: step & (step - 1) != 0):
        top = 1 << (step.bit_length() - 1)
        low = step ^ top
        firsts[step] = (
            swap(firsts[top], "bas", n_bas, low) if low else swap(message, "bas", n_bas, top)
        )
    metas = [got[: meta.shape[0], basis : basis + slots].astype(jnp.int32) for got in firsts]

    part = rows // (n_bas * n_orb)
    live = jnp.arange(slots) < after(counts, message)[0, 0]

    def chunk(dest):
        taken = lax.dynamic_slice_in_dim(tiles, (dest * n_orb + orb) * part, part, 1)
        return jnp.where(live[:, None, None], taken, 0)

    seconds = [None, swap(firsts[1], "aux", n_aux)]
    for step in range(2, n_bas):
        seconds.append(swap(after(firsts[step], seconds[-1]), "aux", n_aux))
    arrived = [chunk(bas)]
    for step in range(1, n_bas):
        gate = firsts[1] if step == n_bas // 2 else seconds[1]
        arrived.append(swap(after(chunk(bas ^ step), gate), "bas", n_bas, step))
    pieces = [[coeff]]
    for step in range(1, n_bas):
        pieces.append([firsts[step], seconds[step]])
    metas = jnp.stack(metas)

    def select(where_ref, meta_ref, *refs):
        groups, at = [], 0
        for piece in pieces:
            groups.append(refs[at : at + len(piece)])
            at += len(piece)
        select_kernel(n_bas, basis // width, where_ref, meta_ref, *groups, *refs[at:])

    flat = [x for piece in pieces for x in piece]
    sizes = cut(n_bas * slots, PIECES)
    mine = pl.pallas_call(
        select,
        out_shape=[jax.ShapeDtypeStruct((size, count, width), coeff.dtype) for size in sizes],
        in_specs=[smem(), smem()] + [vmem()] * len(flat),
        out_specs=[vmem()] * len(sizes),
        scratch_shapes=[pltpu.VMEM((n_bas, count, basis), coeff.dtype)],
        compiler_params=params,
        name="select",
    )(where, metas, *flat)
    other = [swap(part, "orb", n_orb) for part in mine]

    strip = jax.ShapeDtypeStruct((n_bas, ROWS, n_aux * ROWS), jnp.float32)
    keep, send = pl.pallas_call(
        functools.partial(exchange_kernel, n_bas, n_aux, n_orb),
        out_shape=(strip, strip),
        in_specs=[smem(), smem()] + [vmem()] * (n_bas + 2 * PIECES),
        out_specs=(vmem(), vmem()),
        scratch_shapes=[
            pltpu.VMEM((PBLK, part // TM, n_bas, ROWS, n_orb * count), jnp.float32),
            pltpu.VMEM((n_bas, ROWS, n_bas * ROWS), jnp.float32),
        ],
        compiler_params=params,
        name="exchange",
    )(where, metas, *arrived, *mine, *other)

    rest = keep[1:] + swap(send[1:], "orb", n_orb)
    strips = [keep[0] + swap(send[0], "orb", n_orb), *rest]
    strip = strips[0]
    for step in sorted(range(1, n_bas), key=lambda step: step != n_bas // 2):
        strip = strip + swap(strips[step], "bas", n_bas, step)
    total = strip[:, :ROWS]
    for step in range(1, n_aux):
        total = total + swap(strip[:, step * ROWS : (step + 1) * ROWS], "aux", n_aux, step)
    return total


def solution(mesh):
    placed = (
        P(("frag", "bas", "aux"), None, None),
        P(("frag", "bas", "aux"), None),
        P(("frag", "bas", "aux"), None),
        P(("frag", "bas"), "orb"),
    )
    sizes = mesh.shape
    return jax.shard_map(
        functools.partial(body, sizes["bas"], sizes["aux"], sizes["orb"]),
        mesh=mesh,
        in_specs=placed,
        out_specs=P(("frag", "bas"), ("aux", "orb")),
        check_vma=False,
    )
```
